128 devices in a mesh: row: 16 (over z, y_hi, core), col: 8 (over y_lo, x).
Axes of the slice: x: 4, y: 4 (y_hi: 2, y_lo: 2; y = y_hi * 2 + y_lo), z: 4, core: 2. Of those that a mesh axis runs over, the one named last changes fastest.
Arguments:
- features: bfloat16 [131072, 64], P(('col', 'row')), may hold values from -6 to 6
- weight: bfloat16 [64, 256], replicated, may hold values from -0.75 to 0.75
- cotangent: bfloat16 [131072, 256], P(('row', 'col')), may hold values from -6 to 6
- tile_values: bfloat16 [16, 8, 384, 128, 128], P('row', 'col'), may hold values from -0.25 to 0.25
- tile_rows: int32 [16, 8, 384], P('row', 'col'), may hold values from 0 to 63
- tile_cols: int32 [16, 8, 384], P('row', 'col'), may hold values from 0 to 127
- tile_counts: int32 [16, 8], P('row', 'col'), may hold values from 1 to 384, as said below
Outputs:
- activations: bfloat16 [131072, 256], P(('row', 'col'))
- feature_grad: bfloat16 [131072, 64], P(('col', 'row'))
- weight_grad: float32 [64, 256], replicated
The draws below stay inside these ranges and needn't reach their ends.
Inputs may be any that keep to these rules, and one draw needn't show every extreme that they name: `tile_counts`: each grid block's number of live tile slots; some grid block uses all 384 slots.
All inputs are finite; a program needn't handle non-finite values.
Results may differ from the reference program's by a relative error of at most 0.006.
Values may be sent and summed in bfloat16 or wider, within the bound.
No kernel may reach another device: no remote copies, remote signals or barrier semaphores. Data moves between devices by JAX's collectives and lax.ppermute only.
A program may use at most 128 MiB of HBM per device.

```python
import jax
import jax.numpy as jnp
from jax import lax

TILE = 128
F = 64
HID = 256
ND = 1024
TILES_DEV = 384
NODES = 131072
N_ROW = 16
N_COL = 8


def draw_tile_counts(key, part):
    key = jax.random.fold_in(key, 5)
    levels = jax.random.randint(key, (N_ROW * N_COL,), 1, 17)
    counts = jnp.maximum(1, levels * levels * TILES_DEV // 256)
    chosen = jax.random.randint(jax.random.fold_in(key, 1), (), 0, N_ROW * N_COL)
    counts = jnp.where(jnp.arange(N_ROW * N_COL) == chosen, TILES_DEV, counts)
    return counts.reshape(N_ROW, N_COL).astype(jnp.int32)


def set_ends(values, own_key, least, top_value):
    longest = values.shape.index(max(values.shape))
    spots = []
    for shift in (0, 1):
        where = [jax.random.randint(jax.random.fold_in(own_key, axis), (), 0, length) for axis, length in enumerate(values.shape)]
        where[longest] = (where[longest] + shift) % values.shape[longest]
        spots.append(tuple(where))
    return values.at[spots[0]].set(least).at[spots[1]].set(top_value)


def block_levels(rng, shape, cuts, smallest, high):
    def one(dim, shards_of):
        heights = jax.random.uniform(jax.random.fold_in(jax.random.fold_in(rng, 6), dim), (shards_of,), jnp.float32, smallest / len(cuts), high / len(cuts))
        return jnp.repeat(jnp.exp(heights), shape[dim] // shards_of).reshape((-1,) + (1,) * (len(shape) - dim - 1))

    level = one(*cuts[0])
    for cut in cuts[1:]:
        level = level * one(*cut)
    return level


def bell_draw(key, extent, scale, bound, cuts=(), kind=jnp.bfloat16):
    entries = scale * jax.random.normal(key, extent, jnp.float32)
    if cuts:
        entries = entries * block_levels(key, extent, cuts, -0.22, 0.18)
    return jnp.clip(entries, -bound, bound).astype(kind)


def setup_inputs(seed: int = 0) -> dict:
    streams_of = jax.random.split(jax.random.key(seed), 8)
    return {
        "features": bell_draw(streams_of[0], (NODES, F), 1.0, 6.0, ((0, 128),)),
        "weight": bell_draw(streams_of[1], (F, HID), F ** -0.5, 0.75),
        "cotangent": bell_draw(streams_of[2], (NODES, HID), 1.0, 6.0, ((0, 128),)),
        "tile_values": bell_draw(streams_of[3], (N_ROW, N_COL, TILES_DEV, TILE, TILE), (1.3 * (ND / TILES_DEV) ** 0.5 / TILE), 0.25, ((0, 16), (1, 8))),
        "tile_rows": set_ends(jax.random.randint(streams_of[4], (N_ROW, N_COL, TILES_DEV), 0, ND * N_COL // TILE), jax.random.fold_in(streams_of[4], 1), 0, (ND * N_COL // TILE) - 1).astype(jnp.int32),
        "tile_cols": set_ends(jax.random.randint(streams_of[5], (N_ROW, N_COL, TILES_DEV), 0, ND * N_ROW // TILE), jax.random.fold_in(streams_of[5], 1), 0, (ND * N_ROW // TILE) - 1).astype(jnp.int32),
        "tile_counts": draw_tile_counts(jax.random.fold_in(streams_of[7], 71), 0),
    }


def spread(source, targets, picks, values, inside, out_tiles, transpose):
    tiled = source.reshape(-1, TILE, F)

    def visit(totals, item):
        block_values, target, pick, keep = item
        picked = tiled[pick].astype(jnp.float32)
        matrices = block_values.astype(jnp.float32)
        if transpose:
            product = jnp.einsum("tji,tjf->tif", matrices, picked)
        else:
            product = jnp.einsum("tij,tjf->tif", matrices, picked)
        product = jnp.where(keep[:, None, None], product, 0.0)
        return totals.at[target].add(product), None

    start = jnp.zeros((out_tiles, TILE, F), jnp.float32)
    totals, unused = lax.scan(visit, start, (values, targets, picks, inside))
    return totals.reshape(-1, F)


def reference(features, weight, cotangent, tile_values, tile_rows, tile_cols, tile_counts):
    grid = N_ROW * N_COL
    out_tiles = ND * N_ROW * N_COL // TILE
    values = tile_values.reshape(grid, TILES_DEV, TILE, TILE)
    rows = tile_rows.reshape(grid, TILES_DEV).astype(jnp.int32)
    cols = tile_cols.reshape(grid, TILES_DEV).astype(jnp.int32)
    counts = tile_counts.reshape(grid).astype(jnp.int32)
    device = jnp.arange(grid, dtype=jnp.int32)
    row_block = device // N_COL
    col_block = device % N_COL
    global_rows = row_block[:, None] * (ND * N_COL // TILE) + rows
    global_cols = col_block[:, None] * (ND * N_ROW // TILE) + cols
    inside = jnp.arange(TILES_DEV, dtype=jnp.int32)[None, :] < counts[:, None]
    aggregated = spread(features, global_rows, global_cols, values, inside, out_tiles, False)
    aggregated_low = aggregated.astype(jnp.bfloat16)
    pre = jnp.dot(aggregated_low, weight, preferred_element_type=jnp.float32)
    activations = jax.nn.silu(pre).astype(jnp.bfloat16)
    sigma = jax.nn.sigmoid(pre)
    pre_grad = (cotangent.astype(jnp.float32) * sigma * (1.0 + pre * (1.0 - sigma))).astype(jnp.bfloat16)
    aggregated_grad = jnp.dot(pre_grad, weight.T, preferred_element_type=jnp.float32).astype(jnp.bfloat16)
    feature_grad = spread(aggregated_grad, global_cols, global_rows, values, inside, out_tiles, True).astype(jnp.bfloat16)
    weight_grad = jnp.dot(aggregated_low.T, pre_grad, preferred_element_type=jnp.float32)
    return activations, feature_grad, weight_grad
```

```python
import functools

import jax
import jax.numpy as jnp
from jax import lax
from jax.experimental import pallas as pl
from jax.experimental.pallas import tpu as pltpu
from jax.sharding import Mesh, PartitionSpec as P

SIDE = 128
GROUP = 16
VMEM_LIMIT = 56 * 1024 * 1024
f32 = jnp.float32
bf16 = jnp.bfloat16

SMEM_SPEC = pl.BlockSpec(memory_space=pltpu.SMEM)
VMEM_SPEC = pl.BlockSpec(memory_space=pltpu.VMEM)
ANY_SPEC = pl.BlockSpec(memory_space=pl.ANY)


def run_tiles(live, targets, picks, values, tiles, total, sems, load, contract):
    groups = (live + GROUP - 1) // GROUP
    dump = total.shape[0] - 1

    def copy(group):
        here = pl.ds(group * GROUP, GROUP)
        return pltpu.make_async_copy(values.at[here], tiles.at[here], sems.at[group])

    def begin(group, carry):
        copy(group).start()
        return carry

    lax.fori_loop(0, groups, begin, 0)
    total[...] = jnp.zeros_like(total)

    def step(group, carry):
        copy(group).wait()
        products = []
        for i in range(GROUP):
            slot = group * GROUP + i
            products.append(
                lax.dot_general(
                    load(picks[0, 0, slot]), tiles[slot], contract, preferred_element_type=f32
                )
            )
        for i in range(GROUP):
            slot = group * GROUP + i
            target = jnp.where(slot < live, targets[0, 0, slot], dump)
            total[target] += products[i]
        return carry

    lax.fori_loop(0, groups, step, 0)


def forward_kernel(count, rows, cols, core, values, own, other, out, tiles, total, source, sems):
    mine = core[0]
    features = own.shape[1]
    for chip in range(own.shape[0]):
        for k in range(own.shape[2] // SIDE):
            lanes = slice(k * SIDE, (k + 1) * SIDE)
            source[chip, mine, k] = own[chip, :, lanes]
            source[chip, 1 - mine, k] = other[chip, :, lanes]

    def load(pick):
        return source[pick // 16, (pick // 8) % 2, pick % 8]

    run_tiles(count[0, 0], rows, cols, values, tiles, total, sems, load, (((1,), (1,)), ((), ())))
    per = out.shape[1] // features
    for tile in range(out.shape[0] * per):
        at = (tile % per) * features
        out[tile // per, at : at + features, :] = total[tile].astype(bf16)


def dense_kernel(parts, weight, cotangent, act, send):
    features = weight.shape[0]
    weight_part = jnp.zeros(weight.shape, f32)
    for k in range(act.shape[0] // SIDE):
        at = slice(k * features, (k + 1) * features)
        nodes = slice(k * SIDE, (k + 1) * SIDE)
        total = parts[0, at, :].astype(f32)
        for s in range(1, parts.shape[0]):
            total = total + parts[s, at, :].astype(f32)
        low = total.astype(bf16)
        pre = lax.dot_general(low, weight[...], (((0,), (0,)), ((), ())), preferred_element_type=f32)
        sigma = 1.0 / (1.0 + jnp.exp(-pre))
        act[nodes, :] = (pre * sigma).astype(bf16)
        grad = (cotangent[nodes, :].astype(f32) * sigma * (1.0 + pre * (1.0 - sigma))).astype(bf16)
        own = lax.dot_general(
            weight[...], grad, (((1,), (1,)), ((), ())), preferred_element_type=f32
        ).astype(bf16)
        for s in range(send.shape[0]):
            send[s, at, :] = own
        weight_part = weight_part + jnp.dot(low, grad, preferred_element_type=f32)
    base = parts.shape[1]
    low = weight_part.astype(bf16)
    for s in range(send.shape[0]):
        for k in range(weight.shape[1] // SIDE):
            send[s, base + k * features : base + (k + 1) * features, :] = low[:, k * SIDE : (k + 1) * SIDE]


def backward_kernel(count, rows, cols, core, values, grads, keep, give, tiles, total, sems):
    mine = core[0]
    chips, rows_each = keep.shape[0], keep.shape[1]
    extra = give.shape[0] - chips * rows_each
    features = rows_each // 8

    def load(pick):
        at = pl.multiple_of((pick % 8) * features, features)
        return grads[pick // 8, pl.ds(at, features), :]

    run_tiles(count[0, 0], cols, rows, values, tiles, total, sems, load, (((1,), (0,)), ((), ())))
    for chip in range(chips):
        for k in range(8):
            at = k * features
            keep[chip, at : at + features, :] = total[chip * 16 + mine * 8 + k]
            at = chip * rows_each + k * features
            give[at : at + features, :] = total[chip * 16 + (1 - mine) * 8 + k].astype(bf16)
    weight = grads[0, rows_each:, :].astype(f32)
    for s in range(1, grads.shape[0]):
        weight = weight + grads[s, rows_each:, :].astype(f32)
    give[chips * rows_each : chips * rows_each + extra, :] = weight.astype(bf16)


def pair_kernel(keep, give, got, send):
    chips, rows_each = keep.shape[0], keep.shape[1]
    for chip in range(chips):
        at = slice(chip * rows_each, (chip + 1) * rows_each)
        send[chip, :rows_each, :] = (keep[chip] + got[at, :].astype(f32)).astype(bf16)
    at = chips * rows_each
    weight = (give[at:, :].astype(f32) + got[at:, :].astype(f32)).astype(bf16)
    for chip in range(chips):
        send[chip, rows_each:, :] = weight


def last_kernel(parts, grad, weight_grad):
    features = grad.shape[0]
    for k in range(grad.shape[1] // SIDE):
        at = slice(k * features, (k + 1) * features)
        total = parts[0, at, :].astype(f32)
        for s in range(1, parts.shape[0]):
            total = total + parts[s, at, :].astype(f32)
        grad[:, k * SIDE : (k + 1) * SIDE] = total.astype(bf16)
    base = grad.shape[1] // SIDE * features
    for k in range(weight_grad.shape[1] // SIDE):
        at = slice(base + k * features, base + (k + 1) * features)
        total = parts[0, at, :].astype(f32)
        for s in range(1, parts.shape[0]):
            total = total + parts[s, at, :].astype(f32)
        weight_grad[:, k * SIDE : (k + 1) * SIDE] = total


def call(kernel, out_shape, in_specs, scratch=()):
    return pl.pallas_call(
        kernel,
        out_shape=out_shape,
        in_specs=in_specs,
        out_specs=jax.tree.map(lambda _: VMEM_SPEC, out_shape),
        scratch_shapes=scratch,
        compiler_params=pltpu.CompilerParams(vmem_limit_bytes=VMEM_LIMIT),
    )


def on_device(features, weight, cotangent, tile_values, tile_rows, tile_cols, tile_counts):
    nodes, width = features.shape
    hidden = weight.shape[1]
    slots = tile_values.shape[2]
    values = tile_values.reshape(slots, SIDE, SIDE)
    chips, cols = lax.axis_size("zy"), lax.axis_size("col")
    core = lax.axis_index("core").astype(jnp.int32).reshape(1)
    swap = [(0, 1), (1, 0)]
    shape = jax.ShapeDtypeStruct
    tiles_each = nodes // SIDE
    rows_each = tiles_each * width
    extra = hidden // SIDE * width

    own = lax.all_to_all(
        jnp.broadcast_to(features.T[None], (chips, width, nodes)), "zy", 0, 0, tiled=True
    )
    other = lax.ppermute(own, "core", swap)

    row_tiles, col_tiles = cols * tiles_each, 2 * chips * tiles_each
    tiles = pltpu.VMEM((slots, SIDE, SIDE), bf16)
    sems = pltpu.SemaphoreType.DMA((slots // GROUP,))
    partial = call(
        forward_kernel,
        shape((cols, rows_each, SIDE), bf16),
        [SMEM_SPEC] * 4 + [ANY_SPEC] + [VMEM_SPEC] * 2,
        [
            tiles,
            pltpu.VMEM((row_tiles + 1, width, SIDE), f32),
            pltpu.VMEM((chips, 2, tiles_each, width, SIDE), bf16),
            sems,
        ],
    )(tile_counts, tile_rows, tile_cols, core, values, own, other)

    parts = lax.all_to_all(partial, "col", 0, 0, tiled=True)
    activations, send = call(
        dense_kernel,
        (shape((nodes, hidden), bf16), shape((cols, rows_each + extra, SIDE), bf16)),
        [VMEM_SPEC] * 3,
    )(parts, weight, cotangent)

    grads = lax.all_to_all(send, "col", 0, 0, tiled=True)
    keep, give = call(
        backward_kernel,
        (shape((chips, rows_each, SIDE), f32), shape((chips * rows_each + extra, SIDE), bf16)),
        [SMEM_SPEC] * 4 + [ANY_SPEC] + [VMEM_SPEC],
        [tiles, pltpu.VMEM((col_tiles + 1, width, SIDE), f32), sems],
    )(tile_counts, tile_rows, tile_cols, core, values, grads)

    got = lax.ppermute(give, "core", swap)
    send = call(pair_kernel, shape((chips, rows_each + extra, SIDE), bf16), [VMEM_SPEC] * 3)(keep, give, got)
    parts = lax.all_to_all(send, "zy", 0, 0, tiled=True)
    grad, weight_grad = call(
        last_kernel,
        (shape((width, nodes), bf16), shape((width, hidden), f32)),
        [VMEM_SPEC],
    )(parts)
    return activations, grad.T, weight_grad


def solution(mesh):
    rows, cols = mesh.shape["row"], mesh.shape["col"]
    split = Mesh(mesh.devices.reshape(rows // 2, 2, cols), ("zy", "core", "col"))
    row = ("zy", "core")
    by_row = ("zy", "core", "col")
    by_col = ("col", "zy", "core")
    in_specs = (
        P(by_col, None),
        P(),
        P(by_row, None),
        P(row, "col", None, None, None),
        P(row, "col", None),
        P(row, "col", None),
        P(row, "col"),
    )
    out_specs = (P(by_row, None), P(by_col, None), P())
    return jax.shard_map(
        on_device, mesh=split, in_specs=in_specs, out_specs=out_specs, check_vma=False
    )
```

```python
import functools

import jax
import jax.numpy as jnp
from jax import lax
from jax.experimental import pallas as pl
from jax.experimental.pallas import tpu as pltpu
from jax.sharding import Mesh, PartitionSpec as P

SIDE = 128
GROUP = 64
MIB = 1024 * 1024
f32 = jnp.float32
bf16 = jnp.bfloat16

SMEM_SPEC = pl.BlockSpec(memory_space=pltpu.SMEM)
VMEM_SPEC = pl.BlockSpec(memory_space=pltpu.VMEM)


def run_tiles(live, targets, values, total, product):
    dump = total.shape[0] - 1
    total[...] = jnp.zeros_like(total)

    def step(group, carry):
        products = [product(group * GROUP + i) for i in range(GROUP)]
        for i in range(GROUP):
            slot = group * GROUP + i
            target = jnp.where(slot < live, targets[0, 0, slot], dump)
            total[target] += products[i]
        return carry

    lax.fori_loop(0, (live + GROUP - 1) // GROUP, step, 0)


def forward_kernel(count, rows, cols, core, values, own, other, out, total, source):
    mine = core[0]
    features = own.shape[1]
    for chip in range(own.shape[0]):
        for k in range(own.shape[2] // SIDE):
            lanes = slice(k * SIDE, (k + 1) * SIDE)
            source[chip * 16 + mine * 8 + k] = own[chip, :, lanes]
            source[chip * 16 + (1 - mine) * 8 + k] = other[chip, :, lanes]

    def product(slot):
        return lax.dot_general(
            values[slot], source[cols[0, 0, slot]], (((1,), (1,)), ((), ())), preferred_element_type=f32
        )

    run_tiles(count[0, 0], rows, values, total, product)
    per = out.shape[1] // features
    for tile in range(out.shape[0] * per):
        at = (tile % per) * features
        out[tile // per, at : at + features, :] = total[tile].T.astype(bf16)


def dense_kernel(parts, weight, cotangent, act, send):
    features = weight.shape[0]
    weight_part = jnp.zeros(weight.shape, f32)
    for k in range(act.shape[0] // SIDE):
        at = slice(k * features, (k + 1) * features)
        nodes = slice(k * SIDE, (k + 1) * SIDE)
        total = parts[0, at, :].astype(f32)
        for s in range(1, parts.shape[0]):
            total = total + parts[s, at, :].astype(f32)
        low = total.astype(bf16)
        pre = lax.dot_general(low, weight[...], (((0,), (0,)), ((), ())), preferred_element_type=f32)
        sigma = 1.0 / (1.0 + jnp.exp(-pre))
        act[nodes, :] = (pre * sigma).astype(bf16)
        grad = (cotangent[nodes, :].astype(f32) * sigma * (1.0 + pre * (1.0 - sigma))).astype(bf16)
        own = lax.dot_general(
            weight[...], grad, (((1,), (1,)), ((), ())), preferred_element_type=f32
        ).astype(bf16)
        for s in range(send.shape[0]):
            send[s, at, :] = own
        weight_part = weight_part + jnp.dot(low, grad, preferred_element_type=f32)
    base = parts.shape[1]
    low = weight_part.astype(bf16)
    for s in range(send.shape[0]):
        for k in range(weight.shape[1] // SIDE):
            send[s, base + k * features : base + (k + 1) * features, :] = low[:, k * SIDE : (k + 1) * SIDE]


def backward_kernel(count, rows, cols, core, values, grads, keep, give, total):
    mine = core[0]
    chips, rows_each = keep.shape[0], keep.shape[1]
    extra = give.shape[0] - chips * rows_each
    features = rows_each // 8

    def product(slot):
        pick = rows[0, 0, slot]
        at = pl.multiple_of((pick % 8) * features, features)
        return jnp.dot(grads[pick // 8, pl.ds(at, features), :], values[slot], preferred_element_type=f32)

    run_tiles(count[0, 0], cols, values, total, product)
    for chip in range(chips):
        for k in range(8):
            at = k * features
            keep[chip, at : at + features, :] = total[chip * 16 + mine * 8 + k]
            at = chip * rows_each + k * features
            give[at : at + features, :] = total[chip * 16 + (1 - mine) * 8 + k].astype(bf16)
    weight = grads[0, rows_each:, :].astype(f32)
    for s in range(1, grads.shape[0]):
        weight = weight + grads[s, rows_each:, :].astype(f32)
    give[chips * rows_each : chips * rows_each + extra, :] = weight.astype(bf16)


def pair_kernel(keep, give, got, send):
    chips, rows_each = keep.shape[0], keep.shape[1]
    for chip in range(chips):
        at = slice(chip * rows_each, (chip + 1) * rows_each)
        send[chip, :rows_each, :] = (keep[chip] + got[at, :].astype(f32)).astype(bf16)
    at = chips * rows_each
    weight = (give[at:, :].astype(f32) + got[at:, :].astype(f32)).astype(bf16)
    for chip in range(chips):
        send[chip, rows_each:, :] = weight


def last_kernel(parts, grad, weight_grad):
    features = grad.shape[0]
    for k in range(grad.shape[1] // SIDE):
        at = slice(k * features, (k + 1) * features)
        total = parts[0, at, :].astype(f32)
        for s in range(1, parts.shape[0]):
            total = total + parts[s, at, :].astype(f32)
        grad[:, k * SIDE : (k + 1) * SIDE] = total.astype(bf16)
    base = grad.shape[1] // SIDE * features
    for k in range(weight_grad.shape[1] // SIDE):
        at = slice(base + k * features, base + (k + 1) * features)
        total = parts[0, at, :].astype(f32)
        for s in range(1, parts.shape[0]):
            total = total + parts[s, at, :].astype(f32)
        weight_grad[:, k * SIDE : (k + 1) * SIDE] = total


def call(kernel, out_shape, scalars, arrays, scratch=(), limit=8):
    arrays = [pltpu.with_memory_space_constraint(x, pltpu.VMEM) for x in arrays]
    return pl.pallas_call(
        kernel,
        out_shape=out_shape,
        in_specs=[SMEM_SPEC] * len(scalars) + [VMEM_SPEC] * len(arrays),
        out_specs=jax.tree.map(lambda _: VMEM_SPEC, out_shape),
        scratch_shapes=scratch,
        compiler_params=pltpu.CompilerParams(vmem_limit_bytes=limit * MIB),
    )(*scalars, *arrays)


def on_device(features, weight, cotangent, tile_values, tile_rows, tile_cols, tile_counts):
    nodes, width = features.shape
    hidden = weight.shape[1]
    slots = tile_values.shape[2]
    values = tile_values.reshape(slots, SIDE, SIDE)
    chips, cols = lax.axis_size("zy"), lax.axis_size("col")
    core = lax.axis_index("core").astype(jnp.int32).reshape(1)
    swap = [(0, 1), (1, 0)]
    shape = jax.ShapeDtypeStruct
    tiles_each = nodes // SIDE
    rows_each = tiles_each * width
    extra = hidden // SIDE * width

    own = lax.all_to_all(
        jnp.broadcast_to(features.T[None], (chips, width, nodes)), "zy", 0, 0, tiled=True
    )
    other = lax.ppermute(own, "core", swap)

    row_tiles, col_tiles = cols * tiles_each, 2 * chips * tiles_each
    scalars = (tile_counts, tile_rows, tile_cols, core)
    partial = call(
        forward_kernel,
        shape((cols, rows_each, SIDE), bf16),
        scalars,
        (values, own, other),
        [
            pltpu.VMEM((row_tiles + 1, SIDE, width), f32),
            pltpu.VMEM((col_tiles, width, SIDE), bf16),
        ],
        limit=12,
    )

    parts = lax.all_to_all(partial, "col", 0, 0, tiled=True)
    activations, send = call(
        dense_kernel,
        (shape((nodes, hidden), bf16), shape((cols, rows_each + extra, SIDE), bf16)),
        (),
        (parts, weight, cotangent),
    )

    grads = lax.all_to_all(send, "col", 0, 0, tiled=True)
    keep, give = call(
        backward_kernel,
        (shape((chips, rows_each, SIDE), f32), shape((chips * rows_each + extra, SIDE), bf16)),
        scalars,
        (values, grads),
        [pltpu.VMEM((col_tiles + 1, width, SIDE), f32)],
        limit=12,
    )

    got = lax.ppermute(give, "core", swap)
    send = call(pair_kernel, shape((chips, rows_each + extra, SIDE), bf16), (), (keep, give, got))
    parts = lax.all_to_all(send, "zy", 0, 0, tiled=True)
    grad, weight_grad = call(
        last_kernel, (shape((width, nodes), bf16), shape((width, hidden), f32)), (), (parts,)
    )
    return activations, grad.T, weight_grad


def solution(mesh):
    rows, cols = mesh.shape["row"], mesh.shape["col"]
    split = Mesh(mesh.devices.reshape(rows // 2, 2, cols), ("zy", "core", "col"))
    row = ("zy", "core")
    by_row = ("zy", "core", "col")
    by_col = ("col", "zy", "core")
    in_specs = (
        P(by_col, None),
        P(),
        P(by_row, None),
        P(row, "col", None, None, None),
        P(row, "col", None),
        P(row, "col", None),
        P(row, "col"),
    )
    out_specs = (P(by_row, None), P(by_col, None), P())
    return jax.shard_map(
        on_device, mesh=split, in_specs=in_specs, out_specs=out_specs, check_vma=False
    )
```

```python
import functools

import jax
import jax.numpy as jnp
from jax import lax
from jax.experimental import pallas as pl
from jax.experimental.pallas import tpu as pltpu
from jax.sharding import Mesh, PartitionSpec as P

SIDE = 128
GROUP = 64
MIB = 1024 * 1024
f32 = jnp.float32
bf16 = jnp.bfloat16

SMEM_SPEC = pl.BlockSpec(memory_space=pltpu.SMEM)
VMEM_SPEC = pl.BlockSpec(memory_space=pltpu.VMEM)


def spread_kernel(features, out):
    for chip in range(out.shape[0]):
        out[chip] = features[...]


def run_tiles(live, targets, values, total, product):
    dump = total.shape[0] - 1
    total[...] = jnp.zeros_like(total)

    def step(group, carry):
        products = [product(group * GROUP + i) for i in range(GROUP)]
        for i in range(GROUP):
            slot = group * GROUP + i
            target = jnp.where(slot < live, targets[0, 0, slot], dump)
            total[target] += products[i]
        return carry

    lax.fori_loop(0, (live + GROUP - 1) // GROUP, step, 0)


def forward_kernel(count, rows, cols, values, own, other, out, total, source):
    mine = lax.axis_index("core")
    features = own.shape[1]
    for chip in range(own.shape[0]):
        for k in range(own.shape[2] // SIDE):
            lanes = slice(k * SIDE, (k + 1) * SIDE)
            source[chip * 16 + mine * 8 + k] = own[chip, :, lanes]
            source[chip * 16 + (1 - mine) * 8 + k] = other[chip, :, lanes]

    def product(slot):
        return lax.dot_general(
            values[slot], source[cols[0, 0, slot]], (((1,), (1,)), ((), ())), preferred_element_type=f32
        )

    run_tiles(count[0, 0], rows, values, total, product)
    per = out.shape[1] // features
    for tile in range(out.shape[0] * per):
        at = (tile % per) * features
        out[tile // per, at : at + features, :] = total[tile].T.astype(bf16)


def dense_kernel(parts, weight, cotangent, pre_out, send):
    features = weight.shape[0]
    weight_part = jnp.zeros(weight.shape, f32)
    for k in range(pre_out.shape[0] // SIDE):
        at = slice(k * features, (k + 1) * features)
        nodes = slice(k * SIDE, (k + 1) * SIDE)
        total = parts[0, at, :].astype(f32)
        for s in range(1, parts.shape[0]):
            total = total + parts[s, at, :].astype(f32)
        low = total.astype(bf16)
        pre = lax.dot_general(low, weight[...], (((0,), (0,)), ((), ())), preferred_element_type=f32)
        sigma = 1.0 / (1.0 + jnp.exp(-pre))
        pre_out[nodes, :] = pre
        grad = (cotangent[nodes, :].astype(f32) * sigma * (1.0 + pre * (1.0 - sigma))).astype(bf16)
        own = lax.dot_general(
            weight[...], grad, (((1,), (1,)), ((), ())), preferred_element_type=f32
        ).astype(bf16)
        for s in range(send.shape[0]):
            send[s, at, :] = own
        weight_part = weight_part + jnp.dot(low, grad, preferred_element_type=f32)
    base = parts.shape[1]
    low = weight_part.astype(bf16)
    for s in range(send.shape[0]):
        for k in range(weight.shape[1] // SIDE):
            send[s, base + k * features : base + (k + 1) * features, :] = low[:, k * SIDE : (k + 1) * SIDE]


def activation_kernel(pre, act):
    for k in range(act.shape[0] // SIDE):
        nodes = slice(k * SIDE, (k + 1) * SIDE)
        x = pre[nodes, :]
        act[nodes, :] = (x * (1.0 / (1.0 + jnp.exp(-x)))).astype(bf16)


def backward_kernel(count, rows, cols, values, grads, total, give):
    mine = lax.axis_index("core")
    features = total.shape[1]
    rows_each = 8 * features

    def product(slot):
        pick = rows[0, 0, slot]
        at = pl.multiple_of((pick & 7) * features, features)
        return jnp.dot(grads[pick >> 3, pl.ds(at, features), :], values[slot], preferred_element_type=f32)

    run_tiles(count[0, 0], cols, values, total, product)
    chips = total.shape[0] // 16
    for chip in range(chips):
        for k in range(8):
            at = chip * rows_each + k * features
            give[at : at + features, :] = total[chip * 16 + (1 - mine) * 8 + k].astype(bf16)
    weight = grads[0, rows_each:, :].astype(f32)
    for s in range(1, grads.shape[0]):
        weight = weight + grads[s, rows_each:, :].astype(f32)
    give[chips * rows_each :, :] = weight.astype(bf16)


def pair_kernel(total, give, got, send):
    mine = lax.axis_index("core")
    chips, features = send.shape[0], total.shape[1]
    rows_each = 8 * features
    for chip in range(chips):
        for k in range(8):
            at = chip * rows_each + k * features
            pair = total[chip * 16 + mine * 8 + k] + got[at : at + features, :].astype(f32)
            send[chip, k * features : (k + 1) * features, :] = pair.astype(bf16)
    at = chips * rows_each
    weight = (give[at:, :].astype(f32) + got[at:, :].astype(f32)).astype(bf16)
    for chip in range(chips):
        send[chip, rows_each:, :] = weight


def last_kernel(parts, grad, weight_grad):
    features = grad.shape[0]
    for k in range(grad.shape[1] // SIDE):
        at = slice(k * features, (k + 1) * features)
        total = parts[0, at, :].astype(f32)
        for s in range(1, parts.shape[0]):
            total = total + parts[s, at, :].astype(f32)
        grad[:, k * SIDE : (k + 1) * SIDE] = total.astype(bf16)
    base = grad.shape[1] // SIDE * features
    for k in range(weight_grad.shape[1] // SIDE):
        at = slice(base + k * features, base + (k + 1) * features)
        total = parts[0, at, :].astype(f32)
        for s in range(1, parts.shape[0]):
            total = total + parts[s, at, :].astype(f32)
        weight_grad[:, k * SIDE : (k + 1) * SIDE] = total


def call(kernel, out_shape, scalars, arrays, scratch=(), limit=8, cost=None):
    arrays = [pltpu.with_memory_space_constraint(x, pltpu.VMEM) for x in arrays]
    return pl.pallas_call(
        kernel,
        out_shape=out_shape,
        in_specs=[SMEM_SPEC] * len(scalars) + [VMEM_SPEC] * len(arrays),
        out_specs=jax.tree.map(lambda _: VMEM_SPEC, out_shape),
        scratch_shapes=scratch,
        cost_estimate=cost,
        compiler_params=pltpu.CompilerParams(vmem_limit_bytes=limit * MIB),
    )(*scalars, *arrays)


def on_device(features, weight, cotangent, tile_values, tile_rows, tile_cols, tile_counts):
    nodes, width = features.shape
    hidden = weight.shape[1]
    slots = tile_values.shape[2]
    values = tile_values.reshape(slots, SIDE, SIDE)
    chips, cols = lax.axis_size("zy"), lax.axis_size("col")
    swap = [(0, 1), (1, 0)]
    shape = jax.ShapeDtypeStruct
    tiles_each = nodes // SIDE
    rows_each = tiles_each * width
    extra = hidden // SIDE * width

    send = call(
        spread_kernel,
        shape((chips, width, nodes), bf16),
        (),
        (features.T,),
        cost=pl.CostEstimate(flops=10**10, bytes_accessed=4 * 10**7, transcendentals=0),
    )
    own = lax.all_to_all(send, "zy", 0, 0, tiled=True)
    other = lax.ppermute(own, "core", swap)

    row_tiles, col_tiles = cols * tiles_each, 2 * chips * tiles_each
    scalars = (tile_counts, tile_rows, tile_cols)
    partial = call(
        forward_kernel,
        shape((cols, rows_each, SIDE), bf16),
        scalars,
        (values, own, other),
        [
            pltpu.VMEM((row_tiles + 1, SIDE, width), f32),
            pltpu.VMEM((col_tiles, width, SIDE), bf16),
        ],
        limit=12,
    )

    parts = lax.all_to_all(partial, "col", 0, 0, tiled=True)
    pre, send = call(
        dense_kernel,
        (shape((nodes, hidden), f32), shape((cols, rows_each + extra, SIDE), bf16)),
        (),
        (parts, weight, cotangent),
    )

    grads = lax.all_to_all(send, "col", 0, 0, tiled=True)
    total, give = call(
        backward_kernel,
        (
            shape((col_tiles + 1, width, SIDE), f32),
            shape((chips * rows_each + extra, SIDE), bf16),
        ),
        scalars,
        (values, grads),
        limit=12,
    )

    pre, give = lax.optimization_barrier((pre, give))
    got = lax.ppermute(give, "core", swap)
    activations = call(activation_kernel, shape((nodes, hidden), bf16), (), (pre,))
    got, activations = lax.optimization_barrier((got, activations))
    send = call(
        pair_kernel, shape((chips, rows_each + extra, SIDE), bf16), (), (total, give, got)
    )
    parts = lax.all_to_all(send, "zy", 0, 0, tiled=True)
    grad, weight_grad = call(
        last_kernel, (shape((width, nodes), bf16), shape((width, hidden), f32)), (), (parts,)
    )
    return activations, grad.T, weight_grad


def solution(mesh):
    rows, cols = mesh.shape["row"], mesh.shape["col"]
    split = Mesh(mesh.devices.reshape(rows // 2, 2, cols), ("zy", "core", "col"))
    row = ("zy", "core")
    by_row = ("zy", "core", "col")
    by_col = ("col", "zy", "core")
    in_specs = (
        P(by_col, None),
        P(),
        P(by_row, None),
        P(row, "col", None, None, None),
        P(row, "col", None),
        P(row, "col", None),
        P(row, "col"),
    )
    out_specs = (P(by_row, None), P(by_col, None), P())
    return jax.shard_map(
        on_device, mesh=split, in_specs=in_specs, out_specs=out_specs, check_vma=False
    )
```

```python
import functools

import jax
import jax.numpy as jnp
from jax import lax
from jax.experimental import pallas as pl
from jax.experimental.pallas import tpu as pltpu
from jax.sharding import Mesh, PartitionSpec as P

SIDE = 128
GROUP = 192
LAG = 8
MIB = 1024 * 1024
f32 = jnp.float32
bf16 = jnp.bfloat16

SMEM_SPEC = pl.BlockSpec(memory_space=pltpu.SMEM)
VMEM_SPEC = pl.BlockSpec(memory_space=pltpu.VMEM)


def spread_kernel(features, out):
    for chip in range(out.shape[0]):
        out[chip] = features[...]


def run_tiles(live, targets, values, total, product):
    dump = total.shape[0] - 1
    total[...] = jnp.zeros_like(total)

    def step(group, carry):
        products = []
        for i in range(GROUP + LAG):
            if i < GROUP:
                products.append(product(group * GROUP + i))
            if i >= LAG:
                slot = group * GROUP + i - LAG
                target = jnp.where(slot < live, targets[0, 0, slot], dump)
                total[target] += products[i - LAG]
        return carry

    lax.fori_loop(0, (live + GROUP - 1) // GROUP, step, 0)


def forward_kernel(count, rows, cols, values, own, other, out, total, source):
    mine = lax.axis_index("core")
    features = own.shape[1]
    for chip in range(own.shape[0]):
        for k in range(own.shape[2] // SIDE):
            lanes = slice(k * SIDE, (k + 1) * SIDE)
            source[chip * 16 + mine * 8 + k] = own[chip, :, lanes]
            source[chip * 16 + (1 - mine) * 8 + k] = other[chip, :, lanes]

    def product(slot):
        return lax.dot_general(
            values[slot], source[cols[0, 0, slot]], (((1,), (1,)), ((), ())), preferred_element_type=f32
        )

    run_tiles(count[0, 0], rows, values, total, product)
    per = out.shape[1] // features
    for tile in range(out.shape[0] * per):
        at = (tile % per) * features
        out[tile // per, at : at + features, :] = total[tile].T.astype(bf16)


def dense_kernel(parts, weight, cotangent, pre_out, send):
    features = weight.shape[0]
    weight_part = jnp.zeros(weight.shape, f32)
    for k in range(pre_out.shape[0] // SIDE):
        at = slice(k * features, (k + 1) * features)
        nodes = slice(k * SIDE, (k + 1) * SIDE)
        total = parts[0, at, :].astype(f32)
        for s in range(1, parts.shape[0]):
            total = total + parts[s, at, :].astype(f32)
        low = total.astype(bf16)
        pre = lax.dot_general(low, weight[...], (((0,), (0,)), ((), ())), preferred_element_type=f32)
        sigma = 1.0 / (1.0 + jnp.exp(-pre))
        pre_out[nodes, :] = pre
        grad = (cotangent[nodes, :].astype(f32) * sigma * (1.0 + pre * (1.0 - sigma))).astype(bf16)
        own = lax.dot_general(
            weight[...], grad, (((1,), (1,)), ((), ())), preferred_element_type=f32
        ).astype(bf16)
        for s in range(send.shape[0]):
            send[s, at, :] = own
        weight_part = weight_part + jnp.dot(low, grad, preferred_element_type=f32)
    base = parts.shape[1]
    low = weight_part.astype(bf16)
    for s in range(send.shape[0]):
        for k in range(weight.shape[1] // SIDE):
            send[s, base + k * features : base + (k + 1) * features, :] = low[:, k * SIDE : (k + 1) * SIDE]


def activation_kernel(pre, act):
    for k in range(act.shape[0] // SIDE):
        nodes = slice(k * SIDE, (k + 1) * SIDE)
        x = pre[nodes, :]
        act[nodes, :] = (x * (1.0 / (1.0 + jnp.exp(-x)))).astype(bf16)


def backward_kernel(count, rows, cols, values, grads, total, give):
    mine = lax.axis_index("core")
    features = total.shape[1]
    rows_each = 8 * features

    def product(slot):
        pick = rows[0, 0, slot]
        at = pl.multiple_of((pick & 7) * features, features)
        return jnp.dot(grads[pick >> 3, pl.ds(at, features), :], values[slot], preferred_element_type=f32)

    run_tiles(count[0, 0], cols, values, total, product)
    chips = total.shape[0] // 16
    for chip in range(chips):
        for k in range(8):
            at = chip * rows_each + k * features
            give[at : at + features, :] = total[chip * 16 + (1 - mine) * 8 + k].astype(bf16)
    weight = grads[0, rows_each:, :].astype(f32)
    for s in range(1, grads.shape[0]):
        weight = weight + grads[s, rows_each:, :].astype(f32)
    give[chips * rows_each :, :] = weight.astype(bf16)


def pair_kernel(total, give, got, send):
    mine = lax.axis_index("core")
    chips, features = send.shape[0], total.shape[1]
    rows_each = 8 * features
    for chip in range(chips):
        for k in range(8):
            at = chip * rows_each + k * features
            pair = total[chip * 16 + mine * 8 + k] + got[at : at + features, :].astype(f32)
            send[chip, k * features : (k + 1) * features, :] = pair.astype(bf16)
    at = chips * rows_each
    weight = (give[at:, :].astype(f32) + got[at:, :].astype(f32)).astype(bf16)
    for chip in range(chips):
        send[chip, rows_each:, :] = weight


def last_kernel(parts, grad, weight_grad):
    features = grad.shape[0]
    for k in range(grad.shape[1] // SIDE):
        at = slice(k * features, (k + 1) * features)
        total = parts[0, at, :].astype(f32)
        for s in range(1, parts.shape[0]):
            total = total + parts[s, at, :].astype(f32)
        grad[:, k * SIDE : (k + 1) * SIDE] = total.astype(bf16)
    base = grad.shape[1] // SIDE * features
    for k in range(weight_grad.shape[1] // SIDE):
        at = slice(base + k * features, base + (k + 1) * features)
        total = parts[0, at, :].astype(f32)
        for s in range(1, parts.shape[0]):
            total = total + parts[s, at, :].astype(f32)
        weight_grad[:, k * SIDE : (k + 1) * SIDE] = total


def call(kernel, out_shape, scalars, arrays, scratch=(), limit=8, cost=None):
    arrays = [pltpu.with_memory_space_constraint(x, pltpu.VMEM) for x in arrays]
    return pl.pallas_call(
        kernel,
        out_shape=out_shape,
        in_specs=[SMEM_SPEC] * len(scalars) + [VMEM_SPEC] * len(arrays),
        out_specs=jax.tree.map(lambda _: VMEM_SPEC, out_shape),
        scratch_shapes=scratch,
        cost_estimate=cost,
        compiler_params=pltpu.CompilerParams(vmem_limit_bytes=limit * MIB),
    )(*scalars, *arrays)


def on_device(features, weight, cotangent, tile_values, tile_rows, tile_cols, tile_counts):
    nodes, width = features.shape
    hidden = weight.shape[1]
    slots = tile_values.shape[2]
    values = tile_values.reshape(slots, SIDE, SIDE)
    chips, cols = lax.axis_size("zy"), lax.axis_size("col")
    swap = [(0, 1), (1, 0)]
    shape = jax.ShapeDtypeStruct
    tiles_each = nodes // SIDE
    rows_each = tiles_each * width
    extra = hidden // SIDE * width

    send = call(
        spread_kernel,
        shape((chips, width, nodes), bf16),
        (),
        (features.T,),
        cost=pl.CostEstimate(flops=10**10, bytes_accessed=4 * 10**7, transcendentals=0),
    )
    own = lax.all_to_all(send, "zy", 0, 0, tiled=True)
    other = lax.ppermute(own, "core", swap)

    row_tiles, col_tiles = cols * tiles_each, 2 * chips * tiles_each
    scalars = (tile_counts, tile_rows, tile_cols)
    partial = call(
        forward_kernel,
        shape((cols, rows_each, SIDE), bf16),
        scalars,
        (values, own, other),
        [
            pltpu.VMEM((row_tiles + 1, SIDE, width), f32),
            pltpu.VMEM((col_tiles, width, SIDE), bf16),
        ],
        limit=20,
    )

    parts = lax.all_to_all(partial, "col", 0, 0, tiled=True)
    pre, send = call(
        dense_kernel,
        (shape((nodes, hidden), f32), shape((cols, rows_each + extra, SIDE), bf16)),
        (),
        (parts, weight, cotangent),
    )

    grads = lax.all_to_all(send, "col", 0, 0, tiled=True)
    total, give = call(
        backward_kernel,
        (
            shape((col_tiles + 1, width, SIDE), f32),
            shape((chips * rows_each + extra, SIDE), bf16),
        ),
        scalars,
        (values, grads),
        limit=20,
    )

    pre, give = lax.optimization_barrier((pre, give))
    got = lax.ppermute(give, "core", swap)
    activations = call(activation_kernel, shape((nodes, hidden), bf16), (), (pre,))
    got, activations = lax.optimization_barrier((got, activations))
    send = call(
        pair_kernel, shape((chips, rows_each + extra, SIDE), bf16), (), (total, give, got)
    )
    parts = lax.all_to_all(send, "zy", 0, 0, tiled=True)
    grad, weight_grad = call(
        last_kernel, (shape((width, nodes), bf16), shape((width, hidden), f32)), (), (parts,)
    )
    return activations, grad.T, weight_grad


def solution(mesh):
    rows, cols = mesh.shape["row"], mesh.shape["col"]
    split = Mesh(mesh.devices.reshape(rows // 2, 2, cols), ("zy", "core", "col"))
    row = ("zy", "core")
    by_row = ("zy", "core", "col")
    by_col = ("col", "zy", "core")
    in_specs = (
        P(by_col, None),
        P(),
        P(by_row, None),
        P(row, "col", None, None, None),
        P(row, "col", None),
        P(row, "col", None),
        P(row, "col"),
    )
    out_specs = (P(by_row, None), P(by_col, None), P())
    return jax.shard_map(
        on_device, mesh=split, in_specs=in_specs, out_specs=out_specs, check_vma=False
    )
```

```python
import functools

import jax
import jax.numpy as jnp
from jax import lax
from jax.experimental import pallas as pl
from jax.experimental.pallas import tpu as pltpu
from jax.sharding import Mesh, PartitionSpec as P

SIDE = 128
GROUP = 192
LAG = 8
MIB = 1024 * 1024
f32 = jnp.float32
bf16 = jnp.bfloat16

SMEM_SPEC = pl.BlockSpec(memory_space=pltpu.SMEM)
VMEM_SPEC = pl.BlockSpec(memory_space=pltpu.VMEM)


def spread_kernel(features, out):
    for chip in range(out.shape[0]):
        out[chip] = features[...]


def run_tiles(live, targets, values, total, product):
    dump = total.shape[0] - 1
    total[...] = jnp.zeros_like(total)

    def step(group, carry):
        products = []
        for i in range(GROUP + LAG):
            if i < GROUP:
                products.append(product(group * GROUP + i))
            if i >= LAG:
                slot = group * GROUP + i - LAG
                target = jnp.where(slot < live, targets[0, 0, slot], dump)
                total[target] += products[i - LAG]
        return carry

    lax.fori_loop(0, (live + GROUP - 1) // GROUP, step, 0)


def forward_kernel(count, rows, cols, values, own, other, out, total, source):
    mine = lax.axis_index("core")
    features = own.shape[1]
    for chip in range(own.shape[0]):
        for k in range(own.shape[2] // SIDE):
            lanes = slice(k * SIDE, (k + 1) * SIDE)
            source[chip * 16 + mine * 8 + k] = own[chip, :, lanes]
            source[chip * 16 + (1 - mine) * 8 + k] = other[chip, :, lanes]

    def product(slot):
        return lax.dot_general(
            values[slot], source[cols[0, 0, slot]], (((1,), (1,)), ((), ())), preferred_element_type=f32
        )

    run_tiles(count[0, 0], rows, values, total, product)
    per = out.shape[1] // SIDE
    for pair in range(out.shape[0] * per):
        at = (pair % per) * SIDE
        both = jnp.concatenate([total[2 * pair].astype(bf16), total[2 * pair + 1].astype(bf16)], axis=1)
        out[pair // per, at : at + SIDE, :] = both


def dense_kernel(parts, weight, cotangent, pre_out, send):
    features = weight.shape[0]
    weight_part = jnp.zeros(weight.shape, f32)
    for k in range(pre_out.shape[0] // SIDE):
        at = slice(k * features, (k + 1) * features)
        nodes = slice(k * SIDE, (k + 1) * SIDE)
        if k % 2 == 0:
            pair = slice(k // 2 * SIDE, (k // 2 + 1) * SIDE)
            total = parts[0, pair, :].astype(f32)
            for s in range(1, parts.shape[0]):
                total = total + parts[s, pair, :].astype(f32)
            both = total.astype(bf16)
        low = both[:, (k % 2) * features : (k % 2 + 1) * features]
        pre = jnp.dot(low, weight[...], preferred_element_type=f32)
        sigma = 1.0 / (1.0 + jnp.exp(-pre))
        pre_out[nodes, :] = pre
        grad = (cotangent[nodes, :].astype(f32) * sigma * (1.0 + pre * (1.0 - sigma))).astype(bf16)
        own = lax.dot_general(
            weight[...], grad, (((1,), (1,)), ((), ())), preferred_element_type=f32
        ).astype(bf16)
        for s in range(send.shape[0]):
            send[s, at, :] = own
        weight_part = weight_part + lax.dot_general(
            low, grad, (((0,), (0,)), ((), ())), preferred_element_type=f32
        )
    base = parts.shape[1]
    low = weight_part.astype(bf16)
    for s in range(send.shape[0]):
        for k in range(weight.shape[1] // SIDE):
            send[s, base + k * features : base + (k + 1) * features, :] = low[:, k * SIDE : (k + 1) * SIDE]


def activation_kernel(pre, act):
    for k in range(act.shape[0] // SIDE):
        nodes = slice(k * SIDE, (k + 1) * SIDE)
        x = pre[nodes, :]
        act[nodes, :] = (x * (1.0 / (1.0 + jnp.exp(-x)))).astype(bf16)


def backward_kernel(count, rows, cols, values, grads, total, give):
    mine = lax.axis_index("core")
    features = total.shape[1]
    rows_each = 8 * features

    def product(slot):
        pick = rows[0, 0, slot]
        at = pl.multiple_of((pick & 7) * features, features)
        return jnp.dot(grads[pick >> 3, pl.ds(at, features), :], values[slot], preferred_element_type=f32)

    run_tiles(count[0, 0], cols, values, total, product)
    chips = total.shape[0] // 16
    for chip in range(chips):
        for k in range(8):
            at = chip * rows_each + k * features
            give[at : at + features, :] = total[chip * 16 + (1 - mine) * 8 + k].astype(bf16)
    weight = grads[0, rows_each:, :].astype(f32)
    for s in range(1, grads.shape[0]):
        weight = weight + grads[s, rows_each:, :].astype(f32)
    give[chips * rows_each :, :] = weight.astype(bf16)


def pair_kernel(total, give, got, send):
    mine = lax.axis_index("core")
    chips, features = send.shape[0], total.shape[1]
    rows_each = 8 * features
    for chip in range(chips):
        for k in range(8):
            at = chip * rows_each + k * features
            pair = total[chip * 16 + mine * 8 + k] + got[at : at + features, :].astype(f32)
            send[chip, k * features : (k + 1) * features, :] = pair.astype(bf16)
    at = chips * rows_each
    weight = (give[at:, :].astype(f32) + got[at:, :].astype(f32)).astype(bf16)
    for chip in range(chips):
        send[chip, rows_each:, :] = weight


def last_kernel(parts, grad, weight_grad):
    features = grad.shape[0]
    for k in range(grad.shape[1] // SIDE):
        at = slice(k * features, (k + 1) * features)
        total = parts[0, at, :].astype(f32)
        for s in range(1, parts.shape[0]):
            total = total + parts[s, at, :].astype(f32)
        grad[:, k * SIDE : (k + 1) * SIDE] = total.astype(bf16)
    base = grad.shape[1] // SIDE * features
    for k in range(weight_grad.shape[1] // SIDE):
        at = slice(base + k * features, base + (k + 1) * features)
        total = parts[0, at, :].astype(f32)
        for s in range(1, parts.shape[0]):
            total = total + parts[s, at, :].astype(f32)
        weight_grad[:, k * SIDE : (k + 1) * SIDE] = total


def call(kernel, out_shape, scalars, arrays, scratch=(), limit=8, cost=None):
    arrays = [pltpu.with_memory_space_constraint(x, pltpu.VMEM) for x in arrays]
    return pl.pallas_call(
        kernel,
        out_shape=out_shape,
        in_specs=[SMEM_SPEC] * len(scalars) + [VMEM_SPEC] * len(arrays),
        out_specs=jax.tree.map(lambda _: VMEM_SPEC, out_shape),
        scratch_shapes=scratch,
        cost_estimate=cost,
        compiler_params=pltpu.CompilerParams(vmem_limit_bytes=limit * MIB),
    )(*scalars, *arrays)


def on_device(features, weight, cotangent, tile_values, tile_rows, tile_cols, tile_counts):
    nodes, width = features.shape
    hidden = weight.shape[1]
    slots = tile_values.shape[2]
    values = tile_values.reshape(slots, SIDE, SIDE)
    chips, cols = lax.axis_size("zy"), lax.axis_size("col")
    swap = [(0, 1), (1, 0)]
    shape = jax.ShapeDtypeStruct
    tiles_each = nodes // SIDE
    rows_each = tiles_each * width
    extra = hidden // SIDE * width

    send = call(
        spread_kernel,
        shape((chips, width, nodes), bf16),
        (),
        (features.T,),
        cost=pl.CostEstimate(flops=10**10, bytes_accessed=4 * 10**7, transcendentals=0),
    )
    own = lax.all_to_all(send, "zy", 0, 0, tiled=True)
    other = lax.ppermute(own, "core", swap)

    row_tiles, col_tiles = cols * tiles_each, 2 * chips * tiles_each
    scalars = (tile_counts, tile_rows, tile_cols)
    partial = call(
        forward_kernel,
        shape((cols, rows_each, SIDE), bf16),
        scalars,
        (values, own, other),
        [
            pltpu.VMEM((row_tiles + 1, SIDE, width), f32),
            pltpu.VMEM((col_tiles, width, SIDE), bf16),
        ],
        limit=20,
    )

    parts = lax.all_to_all(partial, "col", 0, 0, tiled=True)
    pre, send = call(
        dense_kernel,
        (shape((nodes, hidden), f32), shape((cols, rows_each + extra, SIDE), bf16)),
        (),
        (parts, weight, cotangent),
    )

    grads = lax.all_to_all(send, "col", 0, 0, tiled=True)
    total, give = call(
        backward_kernel,
        (
            shape((col_tiles + 1, width, SIDE), f32),
            shape((chips * rows_each + extra, SIDE), bf16),
        ),
        scalars,
        (values, grads),
        limit=20,
    )

    pre, give = lax.optimization_barrier((pre, give))
    got = lax.ppermute(give, "core", swap)
    activations = call(activation_kernel, shape((nodes, hidden), bf16), (), (pre,))
    got, activations = lax.optimization_barrier((got, activations))
    send = call(
        pair_kernel, shape((chips, rows_each + extra, SIDE), bf16), (), (total, give, got)
    )
    parts = lax.all_to_all(send, "zy", 0, 0, tiled=True)
    grad, weight_grad = call(
        last_kernel, (shape((width, nodes), bf16), shape((width, hidden), f32)), (), (parts,)
    )
    return activations, grad.T, weight_grad


def solution(mesh):
    rows, cols = mesh.shape["row"], mesh.shape["col"]
    split = Mesh(mesh.devices.reshape(rows // 2, 2, cols), ("zy", "core", "col"))
    row = ("zy", "core")
    by_row = ("zy", "core", "col")
    by_col = ("col", "zy", "core")
    in_specs = (
        P(by_col, None),
        P(),
        P(by_row, None),
        P(row, "col", None, None, None),
        P(row, "col", None),
        P(row, "col", None),
        P(row, "col"),
    )
    out_specs = (P(by_row, None), P(by_col, None), P())
    return jax.shard_map(
        on_device, mesh=split, in_specs=in_specs, out_specs=out_specs, check_vma=False
    )
```

```python
import functools

import jax
import jax.numpy as jnp
from jax import lax
from jax.experimental import pallas as pl
from jax.experimental.pallas import tpu as pltpu
from jax.sharding import Mesh, PartitionSpec as P

SIDE = 128
FORWARD, BACKWARD = 384, 192
LAG = 8
MIB = 1024 * 1024
f32 = jnp.float32
bf16 = jnp.bfloat16

SMEM_SPEC = pl.BlockSpec(memory_space=pltpu.SMEM)
VMEM_SPEC = pl.BlockSpec(memory_space=pltpu.VMEM)


def spread_kernel(features, out):
    for chip in range(out.shape[0]):
        out[chip] = features[...]


def run_tiles(live, targets, values, total, product, size):
    dump = total.shape[0] - 1
    total[...] = jnp.zeros_like(total)

    def step(group, carry):
        products = []
        for i in range(size + LAG):
            if i < size:
                products.append(product(group * size + i))
            if i >= LAG:
                slot = group * size + i - LAG
                target = jnp.where(slot < live, targets[0, 0, slot], dump)
                total[target] += products[i - LAG]
        return carry

    lax.fori_loop(0, (live + size - 1) // size, step, 0)


def forward_kernel(count, rows, cols, values, own, other, out, total, source):
    mine = lax.axis_index("core")
    features = own.shape[1]
    for chip in range(own.shape[0]):
        for k in range(own.shape[2] // SIDE):
            lanes = slice(k * SIDE, (k + 1) * SIDE)
            source[chip * 16 + mine * 8 + k] = own[chip, :, lanes]
            source[chip * 16 + (1 - mine) * 8 + k] = other[chip, :, lanes]

    def product(slot):
        return lax.dot_general(
            values[slot], source[cols[0, 0, slot]], (((1,), (1,)), ((), ())), preferred_element_type=f32
        )

    run_tiles(count[0, 0], rows, values, total, product, FORWARD)
    per = out.shape[1] // SIDE
    for pair in range(out.shape[0] * per):
        at = (pair % per) * SIDE
        both = jnp.concatenate([total[2 * pair].astype(bf16), total[2 * pair + 1].astype(bf16)], axis=1)
        out[pair // per, at : at + SIDE, :] = both


def dense_kernel(parts, weight, cotangent, pre_out, send):
    features = weight.shape[0]
    weight_part = jnp.zeros(weight.shape, f32)
    for k in range(pre_out.shape[0] // SIDE):
        at = slice(k * features, (k + 1) * features)
        nodes = slice(k * SIDE, (k + 1) * SIDE)
        if k % 2 == 0:
            pair = slice(k // 2 * SIDE, (k // 2 + 1) * SIDE)
            total = parts[0, pair, :].astype(f32)
            for s in range(1, parts.shape[0]):
                total = total + parts[s, pair, :].astype(f32)
            both = total.astype(bf16)
        low = both[:, (k % 2) * features : (k % 2 + 1) * features]
        pre = jnp.dot(low, weight[...], preferred_element_type=f32)
        sigma = 1.0 / (1.0 + jnp.exp(-pre))
        pre_out[nodes, :] = pre
        grad = (cotangent[nodes, :].astype(f32) * sigma * (1.0 + pre * (1.0 - sigma))).astype(bf16)
        own = lax.dot_general(
            weight[...], grad, (((1,), (1,)), ((), ())), preferred_element_type=f32
        ).astype(bf16)
        for s in range(send.shape[0]):
            send[s, at, :] = own
        weight_part = weight_part + lax.dot_general(
            low, grad, (((0,), (0,)), ((), ())), preferred_element_type=f32
        )
    base = parts.shape[1]
    low = weight_part.astype(bf16)
    for s in range(send.shape[0]):
        for k in range(weight.shape[1] // SIDE):
            send[s, base + k * features : base + (k + 1) * features, :] = low[:, k * SIDE : (k + 1) * SIDE]


def activation_kernel(pre, act):
    for k in range(act.shape[0] // SIDE):
        nodes = slice(k * SIDE, (k + 1) * SIDE)
        x = pre[nodes, :]
        act[nodes, :] = (x * (1.0 / (1.0 + jnp.exp(-x)))).astype(bf16)


def backward_kernel(count, rows, cols, values, grads, total, give):
    mine = lax.axis_index("core")
    features = total.shape[1]
    rows_each = 8 * features

    def product(slot):
        pick = rows[0, 0, slot]
        at = pl.multiple_of((pick & 7) * features, features)
        return jnp.dot(grads[pick >> 3, pl.ds(at, features), :], values[slot], preferred_element_type=f32)

    run_tiles(count[0, 0], cols, values, total, product, BACKWARD)
    chips = total.shape[0] // 16
    for chip in range(chips):
        for k in range(8):
            at = chip * rows_each + k * features
            give[at : at + features, :] = total[chip * 16 + (1 - mine) * 8 + k].astype(bf16)
    weight = grads[0, rows_each:, :].astype(f32)
    for s in range(1, grads.shape[0]):
        weight = weight + grads[s, rows_each:, :].astype(f32)
    give[chips * rows_each :, :] = weight.astype(bf16)


def pair_kernel(total, give, got, send):
    mine = lax.axis_index("core")
    chips, features = send.shape[0], total.shape[1]
    rows_each = 8 * features
    for chip in range(chips):
        for k in range(8):
            at = chip * rows_each + k * features
            pair = total[chip * 16 + mine * 8 + k] + got[at : at + features, :].astype(f32)
            send[chip, k * features : (k + 1) * features, :] = pair.astype(bf16)
    at = chips * rows_each
    weight = (give[at:, :].astype(f32) + got[at:, :].astype(f32)).astype(bf16)
    for chip in range(chips):
        send[chip, rows_each:, :] = weight


def last_kernel(parts, grad, weight_grad):
    features = grad.shape[0]
    for k in range(grad.shape[1] // SIDE):
        at = slice(k * features, (k + 1) * features)
        total = parts[0, at, :].astype(f32)
        for s in range(1, parts.shape[0]):
            total = total + parts[s, at, :].astype(f32)
        grad[:, k * SIDE : (k + 1) * SIDE] = total.astype(bf16)
    base = grad.shape[1] // SIDE * features
    for k in range(weight_grad.shape[1] // SIDE):
        at = slice(base + k * features, base + (k + 1) * features)
        total = parts[0, at, :].astype(f32)
        for s in range(1, parts.shape[0]):
            total = total + parts[s, at, :].astype(f32)
        weight_grad[:, k * SIDE : (k + 1) * SIDE] = total


def call(kernel, out_shape, scalars, arrays, scratch=(), limit=8, cost=None):
    arrays = [pltpu.with_memory_space_constraint(x, pltpu.VMEM) for x in arrays]
    return pl.pallas_call(
        kernel,
        out_shape=out_shape,
        in_specs=[SMEM_SPEC] * len(scalars) + [VMEM_SPEC] * len(arrays),
        out_specs=jax.tree.map(lambda _: VMEM_SPEC, out_shape),
        scratch_shapes=scratch,
        cost_estimate=cost,
        compiler_params=pltpu.CompilerParams(vmem_limit_bytes=limit * MIB),
    )(*scalars, *arrays)


def on_device(features, weight, cotangent, tile_values, tile_rows, tile_cols, tile_counts):
    nodes, width = features.shape
    hidden = weight.shape[1]
    slots = tile_values.shape[2]
    values = tile_values.reshape(slots, SIDE, SIDE)
    chips, cols = lax.axis_size("zy"), lax.axis_size("col")
    swap = [(0, 1), (1, 0)]
    shape = jax.ShapeDtypeStruct
    tiles_each = nodes // SIDE
    rows_each = tiles_each * width
    extra = hidden // SIDE * width

    send = call(
        spread_kernel,
        shape((chips, width, nodes), bf16),
        (),
        (features.T,),
        cost=pl.CostEstimate(flops=10**10, bytes_accessed=4 * 10**7, transcendentals=0),
    )
    own = lax.all_to_all(send, "zy", 0, 0, tiled=True)
    other = lax.ppermute(own, "core", swap)

    row_tiles, col_tiles = cols * tiles_each, 2 * chips * tiles_each
    scalars = (tile_counts, tile_rows, tile_cols)
    partial = call(
        forward_kernel,
        shape((cols, rows_each, SIDE), bf16),
        scalars,
        (values, own, other),
        [
            pltpu.VMEM((row_tiles + 1, SIDE, width), f32),
            pltpu.VMEM((col_tiles, width, SIDE), bf16),
        ],
        limit=20,
    )

    parts = lax.all_to_all(partial, "col", 0, 0, tiled=True)
    pre, send = call(
        dense_kernel,
        (shape((nodes, hidden), f32), shape((cols, rows_each + extra, SIDE), bf16)),
        (),
        (parts, weight, cotangent),
    )

    grads = lax.all_to_all(send, "col", 0, 0, tiled=True)
    total, give = call(
        backward_kernel,
        (
            shape((col_tiles + 1, width, SIDE), f32),
            shape((chips * rows_each + extra, SIDE), bf16),
        ),
        scalars,
        (values, grads),
        limit=20,
    )

    pre, give = lax.optimization_barrier((pre, give))
    got = lax.ppermute(give, "core", swap)
    activations = call(activation_kernel, shape((nodes, hidden), bf16), (), (pre,))
    got, activations = lax.optimization_barrier((got, activations))
    send = call(
        pair_kernel, shape((chips, rows_each + extra, SIDE), bf16), (), (total, give, got)
    )
    parts = lax.all_to_all(send, "zy", 0, 0, tiled=True)
    grad, weight_grad = call(
        last_kernel, (shape((width, nodes), bf16), shape((width, hidden), f32)), (), (parts,)
    )
    return activations, grad.T, weight_grad


def solution(mesh):
    rows, cols = mesh.shape["row"], mesh.shape["col"]
    split = Mesh(mesh.devices.reshape(rows // 2, 2, cols), ("zy", "core", "col"))
    row = ("zy", "core")
    by_row = ("zy", "core", "col")
    by_col = ("col", "zy", "core")
    in_specs = (
        P(by_col, None),
        P(),
        P(by_row, None),
        P(row, "col", None, None, None),
        P(row, "col", None),
        P(row, "col", None),
        P(row, "col"),
    )
    out_specs = (P(by_row, None), P(by_col, None), P())
    return jax.shard_map(
        on_device, mesh=split, in_specs=in_specs, out_specs=out_specs, check_vma=False
    )
```
